32 devices in a mesh: pipe: 4 (over y, x), tensor: 8 (over z, core).
Axes of the slice: x: 2, y: 2, z: 4, core: 2. Of those that a mesh axis runs over, the one named last changes fastest.
Arguments:
- inputs: bfloat16 [8, 128, 8192], P(None, None, 'tensor'), may hold values from -60 to 60
- cotangent: bfloat16 [8, 128, 8192], P(None, None, 'tensor'), may hold values from -13 to 13
- norm_gain: float32 [4, 8192], P('pipe', 'tensor'), may hold values from 0.25 to 1.75
- first_factor: bfloat16 [4, 64, 128, 512], P('pipe', 'tensor'), may hold values from -0.35355339 to 0.35355339
- second_factor: bfloat16 [4, 128, 256, 256], P('pipe', 'tensor'), may hold values from -0.25 to 0.25
- third_factor: bfloat16 [4, 128, 256, 256], P('pipe', 'tensor'), may hold values from -0.3125 to 0.3125
- fourth_factor: bfloat16 [4, 64, 512, 128], P('pipe', 'tensor'), may hold values from -0.22097087 to 0.22097087
Outputs:
- section_out: bfloat16 [4, 8, 128, 8192], P('pipe', None, None, 'tensor')
- section_grad: bfloat16 [4, 8, 128, 8192], P('pipe', None, None, 'tensor')
- gain_grad: float32 [4, 8192], P('pipe', 'tensor')
- first_grad: float32 [4, 64, 128, 512], P('pipe', 'tensor')
- second_grad: float32 [4, 128, 256, 256], P('pipe', 'tensor')
- third_grad: float32 [4, 128, 256, 256], P('pipe', 'tensor')
- fourth_grad: float32 [4, 64, 512, 128], P('pipe', 'tensor')
The draws below stay inside these ranges and needn't reach their ends.
All inputs are finite; a program needn't handle non-finite values.
Results may differ from the reference program's by a relative error of at most 0.013.
Values may be sent and summed in bfloat16 or wider, within the bound.
A program may use at most 384 MiB of HBM per device.

```python
import math
import jax
import jax.numpy as jnp
from jax import lax

D = 8192
BLK = 128
TOK = 128
MICRO = 8
NB = 64
EXPAND = 4
Q = 256
SECTIONS = 4


def stream_parts(key):
    key_base = jax.random.fold_in(key, 11)
    key_groups = jax.random.fold_in(key, 12)
    key_rows = jax.random.fold_in(key, 13)
    groups = NB // 2
    group_scale = jnp.power(10.0, jax.random.uniform(key_groups, (MICRO, TOK, groups, 1), jnp.float32, -0.75, 0.75))
    row_scale = jnp.power(10.0, jax.random.uniform(key_rows, (MICRO, TOK, 1, 1), jnp.float32) - 0.5)
    base = jnp.clip(jax.random.normal(key_base, (MICRO, TOK, groups, 2 * BLK), jnp.float32), -3.0, 3.0)
    return (base, group_scale, row_scale)


def draw_inputs(key, part):
    base, group_scale, row_scale = stream_parts(key)
    return (base * group_scale * row_scale).reshape(MICRO, TOK, D).astype(jnp.bfloat16)


def draw_cotangent(key, part):
    base, group_scale, row_scale = stream_parts(key)
    key_noise = jax.random.fold_in(key, 14)
    noise = jnp.clip(jax.random.normal(key_noise, (MICRO, TOK, D), jnp.float32), -4.0, 4.0)
    shared = (0.5 * base * group_scale).reshape(MICRO, TOK, D)
    return (shared + noise).astype(jnp.bfloat16)


def clipped_normal(key, shape):
    return jnp.clip(jax.random.normal(key, shape, jnp.float32), -3.0, 3.0)


def outer_base(key):
    return clipped_normal(jax.random.fold_in(key, 21), (SECTIONS, NB, BLK, EXPAND * BLK))


def middle_base(key):
    return clipped_normal(jax.random.fold_in(key, 31), (SECTIONS, BLK, Q, Q))


def draw_first_factor(key, part):
    return (outer_base(key) * BLK ** (-0.5)).astype(jnp.bfloat16)


def draw_fourth_factor(key, part):
    tied = jnp.swapaxes(outer_base(key), 2, 3)
    fresh = clipped_normal(jax.random.fold_in(key, 22), (SECTIONS, NB, EXPAND * BLK, BLK))
    return ((0.8 * tied + 0.6 * fresh) * (EXPAND * BLK) ** (-0.5)).astype(jnp.bfloat16)


def draw_second_factor(key, part):
    return (middle_base(key) * Q ** (-0.5)).astype(jnp.bfloat16)


def draw_third_factor(key, part):
    tied = jnp.swapaxes(middle_base(key), 2, 3)
    fresh = clipped_normal(jax.random.fold_in(key, 32), (SECTIONS, BLK, Q, Q))
    return ((0.8 * tied + 0.6 * fresh) * Q ** (-0.5)).astype(jnp.bfloat16)


def setup_inputs(seed: int = 0) -> dict:
    streams_of = jax.random.split(jax.random.key(seed), 8)
    return {
        "inputs": draw_inputs(jax.random.fold_in(streams_of[7], 71), 0),
        "cotangent": draw_cotangent(jax.random.fold_in(streams_of[7], 71), 0),
        "norm_gain": jnp.clip(1.0 + 0.15 * jax.random.normal(streams_of[2], (SECTIONS, D), jnp.float32), 0.25, 1.75),
        "first_factor": draw_first_factor(jax.random.fold_in(streams_of[7], 71), 0),
        "second_factor": draw_second_factor(jax.random.fold_in(streams_of[7], 71), 0),
        "third_factor": draw_third_factor(jax.random.fold_in(streams_of[7], 71), 0),
        "fourth_factor": draw_fourth_factor(jax.random.fold_in(streams_of[7], 71), 0),
    }


EPS = 1e-05
TANH_SCALE = math.sqrt(2.0 / math.pi)
CUBIC_COEF = 0.044715

def gelu_pair(preact):
    tanh_val = jnp.tanh(TANH_SCALE * (preact + CUBIC_COEF * preact * preact * preact))
    gelu_value = 0.5 * preact * (1.0 + tanh_val)
    gelu_slope = 0.5 * (1.0 + tanh_val) + 0.5 * preact * (1.0 - tanh_val * tanh_val) * TANH_SCALE * (1.0 + 3.0 * CUBIC_COEF * preact * preact)
    return (gelu_value, gelu_slope)

def as_float(values):
    return values.astype(jnp.float32)

def factors_of(first_w, second_w, third_w, fourth_w):
    return (as_float(first_w.reshape(NB, BLK, EXPAND, BLK)), as_float(second_w.reshape(BLK, NB, EXPAND, Q)), as_float(third_w.reshape(BLK, Q, NB, EXPAND)), as_float(fourth_w.reshape(NB, EXPAND, BLK, BLK)))

def forward_section(stream_in, gain_row, factors):
    factor_one, factor_two, factor_three, factor_four = factors
    stream = as_float(stream_in)
    inv_rms = lax.rsqrt(lax.optimization_barrier(jnp.mean(stream * stream, axis=-1, keepdims=True)) + EPS)
    normed = (stream * inv_rms * gain_row).astype(jnp.bfloat16)
    spread = jnp.einsum('tij,ijak->tiak', as_float(normed.reshape(TOK, NB, BLK)), factor_one).astype(jnp.bfloat16)
    preact = jnp.einsum('tiac,ciae->tce', as_float(spread), factor_two)
    gelu_value, gelu_slope = gelu_pair(preact)
    activated = gelu_value.astype(jnp.bfloat16)
    mixed = jnp.einsum('tce,ceia->tiac', as_float(activated), factor_three).astype(jnp.bfloat16)
    branch = jnp.einsum('tiak,iakj->tij', as_float(mixed), factor_four).reshape(TOK, D)
    result = (stream + branch).astype(jnp.bfloat16)
    return (result, (stream, inv_rms, normed, spread, activated, gelu_slope, mixed))

def backward_section(grad_out, record, gain_row, factors):
    factor_one, factor_two, factor_three, factor_four = factors
    stream, inv_rms, normed, spread, activated, gelu_slope, mixed = record
    grad_blocks = as_float(grad_out.reshape(TOK, NB, BLK))
    part_four = jnp.einsum('tiak,tij->iakj', as_float(mixed), grad_blocks)
    grad_mixed = jnp.einsum('tij,iakj->tiak', grad_blocks, factor_four).astype(jnp.bfloat16)
    part_three = jnp.einsum('tce,tiac->ceia', as_float(activated), as_float(grad_mixed))
    grad_act = jnp.einsum('tiac,ceia->tce', as_float(grad_mixed), factor_three)
    grad_pre = (grad_act * gelu_slope).astype(jnp.bfloat16)
    part_two = jnp.einsum('tiac,tce->ciae', as_float(spread), as_float(grad_pre))
    grad_spread = jnp.einsum('tce,ciae->tiac', as_float(grad_pre), factor_two).astype(jnp.bfloat16)
    part_one = jnp.einsum('tij,tiak->ijak', as_float(normed.reshape(TOK, NB, BLK)), as_float(grad_spread))
    grad_norm = jnp.einsum('tiak,ijak->tij', as_float(grad_spread), factor_one).reshape(TOK, D)
    part_gain = lax.optimization_barrier(jnp.sum(grad_norm * stream * inv_rms, axis=0))
    scaled_grad = grad_norm * gain_row
    inner_sum = lax.optimization_barrier(jnp.sum(scaled_grad * stream, axis=-1, keepdims=True))
    grad_in = (as_float(grad_out) + scaled_grad * inv_rms - stream * inv_rms * inv_rms * inv_rms * inner_sum / D).astype(jnp.bfloat16)
    parts = (part_gain, part_one.reshape(NB, BLK, EXPAND * BLK), part_two.reshape(BLK, Q, Q), part_three.reshape(BLK, Q, Q), part_four.reshape(NB, EXPAND * BLK, BLK))
    return (grad_in, parts)

def reference(inputs, cotangent, norm_gain, first_factor, second_factor, third_factor, fourth_factor):
    outs_list = [[None] * MICRO for section_id in range(SECTIONS)]
    grads_list = [[None] * MICRO for section_id in range(SECTIONS)]
    totals = [[jnp.zeros((D,), jnp.float32), jnp.zeros((NB, BLK, EXPAND * BLK), jnp.float32), jnp.zeros((BLK, Q, Q), jnp.float32), jnp.zeros((BLK, Q, Q), jnp.float32), jnp.zeros((NB, EXPAND * BLK, BLK), jnp.float32)] for section_id in range(SECTIONS)]
    for micro_id in range(MICRO):
        stream_in = inputs[micro_id]
        records = []
        for section_id in range(SECTIONS):
            factors = factors_of(first_factor[section_id], second_factor[section_id], third_factor[section_id], fourth_factor[section_id])
            result, record = forward_section(stream_in, norm_gain[section_id], factors)
            outs_list[section_id][micro_id] = result
            records.append(record)
            stream_in = result
        grad_out = cotangent[micro_id]
        for section_id in reversed(range(SECTIONS)):
            factors = factors_of(first_factor[section_id], second_factor[section_id], third_factor[section_id], fourth_factor[section_id])
            grad_in, parts = backward_section(grad_out, records[section_id], norm_gain[section_id], factors)
            grads_list[section_id][micro_id] = grad_in
            totals[section_id] = [total + member for total, member in zip(totals[section_id], parts)]
            grad_out = grad_in
    section_out = jnp.stack([jnp.stack(row) for row in outs_list])
    section_grad = jnp.stack([jnp.stack(row) for row in grads_list])
    gain_grad = jnp.stack([totals[section_id][0] for section_id in range(SECTIONS)])
    first_grad = jnp.stack([totals[section_id][1] for section_id in range(SECTIONS)])
    second_grad = jnp.stack([totals[section_id][2] for section_id in range(SECTIONS)])
    third_grad = jnp.stack([totals[section_id][3] for section_id in range(SECTIONS)])
    fourth_grad = jnp.stack([totals[section_id][4] for section_id in range(SECTIONS)])
    return (section_out, section_grad, gain_grad, first_grad, second_grad, third_grad, fourth_grad)
```

```python
import math

import jax
import jax.numpy as jnp
from jax import lax
from jax.sharding import PartitionSpec as P

EPS = 1e-05
TANH_SCALE = math.sqrt(2.0 / math.pi)
CUBIC_COEF = 0.044715
F32 = jnp.float32
BF16 = jnp.bfloat16


def gelu_value(preact):
    tanh_val = jnp.tanh(TANH_SCALE * (preact + CUBIC_COEF * preact * preact * preact))
    return 0.5 * preact * (1.0 + tanh_val)


def gelu_slope(preact):
    tanh_val = jnp.tanh(TANH_SCALE * (preact + CUBIC_COEF * preact * preact * preact))
    return 0.5 * (1.0 + tanh_val) + 0.5 * preact * (
        1.0 - tanh_val * tanh_val
    ) * TANH_SCALE * (1.0 + 3.0 * CUBIC_COEF * preact * preact)


def dot(spec, left, right):
    return jnp.einsum(spec, left, right, preferred_element_type=F32)


def swap(values, axis):
    return lax.all_to_all(values, axis, split_axis=0, concat_axis=0, tiled=True)


def body(inputs, cotangent, norm_gain, first_factor, second_factor, third_factor, fourth_factor):
    sections = lax.axis_size("pipe")
    group = lax.axis_index("pipe")
    ranks = lax.axis_size("tensor")
    rank = lax.axis_index("tensor")
    micro_count, tokens, width_dev = inputs.shape
    width = width_dev * ranks
    share = micro_count // sections
    span = share * tokens
    blocks, block_size = first_factor.shape[1], first_factor.shape[2]
    expand = first_factor.shape[3] // block_size
    cols, mix_width = second_factor.shape[1], second_factor.shape[2]
    all_blocks = mix_width // expand
    inner = expand * cols

    def whole_stream(values):
        mine = lax.dynamic_slice_in_dim(values, group * share, share, 0)
        mine = mine.reshape(span, width_dev).T
        return lax.all_gather(mine, "tensor", axis=0, tiled=True)

    def to_cols(values):
        return (
            values.reshape(all_blocks, expand, cols, span)
            .transpose(2, 0, 1, 3)
            .reshape(cols, mix_width, span)
        )

    def to_blocks(values):
        return (
            values.reshape(cols, all_blocks, expand, span)
            .transpose(1, 2, 0, 3)
            .reshape(all_blocks, inner, span)
        )

    def over_pipe(values):
        return lax.all_gather(values, "pipe", axis=0, tiled=False)

    stream = whole_stream(inputs)
    grad = whole_stream(cotangent)
    gains = over_pipe(lax.all_gather(norm_gain[0], "tensor", axis=0, tiled=True))
    first = first_factor[0].reshape(blocks, block_size, expand, ranks, cols)
    first = first.transpose(3, 0, 2, 4, 1).reshape(ranks * blocks, inner, block_size)
    first = over_pipe(swap(first, "tensor"))
    second = over_pipe(second_factor[0])
    third = over_pipe(third_factor[0])
    fourth = fourth_factor[0].reshape(blocks, expand, ranks, cols, block_size)
    fourth = fourth.transpose(2, 0, 1, 3, 4).reshape(ranks * blocks, inner, block_size)
    fourth = over_pipe(swap(fourth, "tensor"))

    records = []
    outs = []
    for layer in range(sections):
        f = stream.astype(F32)
        inv = lax.rsqrt(jnp.mean(f * f, axis=0) + EPS)
        normed = (f * inv * gains[layer][:, None]).astype(BF16)
        normed = normed.reshape(all_blocks, block_size, span)
        spread = to_cols(dot("ikj,ijt->ikt", first[layer], normed).astype(BF16))
        preact = dot("cme,cmt->cet", second[layer], spread)
        act = gelu_value(preact).astype(BF16)
        mixed = to_blocks(dot("cem,cet->cmt", third[layer], act).astype(BF16))
        branch = dot("ikj,ikt->ijt", fourth[layer], mixed).astype(BF16)
        branch = lax.psum(branch.reshape(width, span), "tensor")
        records.append((stream, inv, normed, spread, preact, act, mixed))
        stream = (f + branch.astype(F32)).astype(BF16)
        outs.append(lax.dynamic_slice_in_dim(stream, rank * width_dev, width_dev, 0))

    def placed(members):
        moved = swap(jnp.stack(members), "pipe")
        moved = moved.reshape(sections, width_dev, share, tokens)
        return moved.transpose(0, 2, 3, 1).reshape(1, micro_count, tokens, width_dev)

    section_out = placed(outs)

    grads = [None] * sections
    parts = [None] * sections
    for layer in reversed(range(sections)):
        stream, inv, normed, spread, preact, act, mixed = records[layer]
        gain = gains[layer][:, None]
        grad_blocks = grad.reshape(all_blocks, block_size, span)
        part_four = dot("ikt,ijt->ikj", mixed, grad_blocks)
        grad_mixed = to_cols(dot("ikj,ijt->ikt", fourth[layer], grad_blocks).astype(BF16))
        part_three = dot("cet,cmt->cem", act, grad_mixed)
        grad_act = dot("cem,cmt->cet", third[layer], grad_mixed)
        grad_pre = (grad_act * gelu_slope(preact)).astype(BF16)
        part_two = dot("cmt,cet->cme", spread, grad_pre)
        grad_spread = to_blocks(dot("cme,cet->cmt", second[layer], grad_pre).astype(BF16))
        part_one = dot("ikt,ijt->ikj", grad_spread, normed)
        grad_norm = dot("ikj,ikt->ijt", first[layer], grad_spread).astype(BF16)
        grad_norm = lax.psum(grad_norm.reshape(width, span), "tensor").astype(F32)
        f = stream.astype(F32)
        my_norm = lax.dynamic_slice_in_dim(grad_norm, rank * width_dev, width_dev, 0)
        my_f = lax.dynamic_slice_in_dim(stream, rank * width_dev, width_dev, 0).astype(F32)
        part_gain = jnp.sum(my_norm * my_f * inv, axis=1)
        scaled = grad_norm * gain
        inner_sum = jnp.sum(scaled * f, axis=0)
        grad = (
            grad.astype(F32) + scaled * inv - f * (inv * inv * inv * inner_sum / width)
        ).astype(BF16)
        grads[layer] = lax.dynamic_slice_in_dim(grad, rank * width_dev, width_dev, 0)
        parts[layer] = (
            part_gain,
            part_one.astype(BF16),
            part_two.astype(BF16),
            part_three.astype(BF16),
            part_four.astype(BF16),
        )

    section_grad = placed(grads)

    def collected(which):
        moved = swap(jnp.stack([part[which] for part in parts]), "pipe")
        return jnp.sum(moved.astype(F32), axis=0)

    def at_home(values):
        values = swap(values.astype(BF16), "tensor")
        return values.reshape(ranks, blocks, expand, cols, block_size).astype(F32)

    gain_grad = collected(0)
    first_grad = at_home(collected(1)).transpose(1, 4, 2, 0, 3)
    fourth_grad = at_home(collected(4)).transpose(1, 2, 0, 3, 4)
    return (
        section_out,
        section_grad,
        gain_grad[None],
        first_grad.reshape(1, blocks, block_size, expand * block_size),
        collected(2)[None],
        collected(3)[None],
        fourth_grad.reshape(1, blocks, expand * block_size, block_size),
    )


def solution(mesh):
    factor = P("pipe", "tensor", None, None)
    stream = P(None, None, "tensor")
    result = P("pipe", None, None, "tensor")
    return jax.shard_map(
        body,
        mesh=mesh,
        in_specs=(stream, stream, P("pipe", "tensor"), factor, factor, factor, factor),
        out_specs=(result, result, P("pipe", "tensor"), factor, factor, factor, factor),
        check_vma=False,
    )
```

```python
import math

import jax
import jax.numpy as jnp
from jax import lax
from jax.experimental.layout import Layout, with_layout_constraint
from jax.sharding import PartitionSpec as P

EPS = 1e-05
TANH_SCALE = math.sqrt(2.0 / math.pi)
CUBIC_COEF = 0.044715
F32 = jnp.float32
BF16 = jnp.bfloat16


def gelu_value(preact):
    tanh_val = jnp.tanh(TANH_SCALE * (preact + CUBIC_COEF * preact * preact * preact))
    return 0.5 * preact * (1.0 + tanh_val)


def gelu_slope(preact):
    tanh_val = jnp.tanh(TANH_SCALE * (preact + CUBIC_COEF * preact * preact * preact))
    return 0.5 * (1.0 + tanh_val) + 0.5 * preact * (
        1.0 - tanh_val * tanh_val
    ) * TANH_SCALE * (1.0 + 3.0 * CUBIC_COEF * preact * preact)


def dot(spec, left, right):
    return jnp.einsum(spec, left, right, preferred_element_type=F32)


def swap(values, axis):
    return lax.all_to_all(values, axis, split_axis=0, concat_axis=0, tiled=True)


def body(inputs, cotangent, norm_gain, first_factor, second_factor, third_factor, fourth_factor):
    sections = lax.axis_size("pipe")
    group = lax.axis_index("pipe")
    ranks = lax.axis_size("tensor")
    rank = lax.axis_index("tensor")
    micro_count, tokens, width_dev = inputs.shape
    width = width_dev * ranks
    share = micro_count // sections
    blocks, block_size = first_factor.shape[1], first_factor.shape[2]
    expand = first_factor.shape[3] // block_size
    cols, mix_width = second_factor.shape[1], second_factor.shape[2]
    all_blocks = mix_width // expand
    inner = expand * cols

    def rows_first(values):
        return with_layout_constraint(values, Layout(major_to_minor=(0, 1)))

    def whole_stream(values):
        mine = lax.dynamic_slice_in_dim(values, group * share, share, 0)
        mine = mine.reshape(share * tokens, width_dev).T
        full = rows_first(lax.all_gather(rows_first(mine), "tensor", axis=0, tiled=True))
        return [full[:, k * tokens : (k + 1) * tokens] for k in range(share)]

    def to_cols(values):
        return (
            values.reshape(all_blocks, expand, cols, tokens)
            .transpose(2, 0, 1, 3)
            .reshape(cols, mix_width, tokens)
        )

    def to_blocks(values):
        return (
            values.reshape(cols, all_blocks, expand, tokens)
            .transpose(1, 2, 0, 3)
            .reshape(all_blocks, inner, tokens)
        )

    def my_rows(values):
        return lax.dynamic_slice_in_dim(values, rank * width_dev, width_dev, 0)

    waiting = [None] * share
    newest = [None]

    def start_sum(k, partial, scatter):
        if newest[0] is not None:
            last = newest[0]
            partial, waiting[last] = lax.optimization_barrier((partial, waiting[last]))
        if scatter:
            waiting[k] = lax.psum_scatter(partial, "tensor", scatter_dimension=0, tiled=True)
        else:
            waiting[k] = rows_first(lax.psum(partial, "tensor"))
        newest[0] = k

    def quarters(values):
        moved = swap(values, "pipe")
        return moved.reshape((sections, moved.shape[0] // sections) + moved.shape[1:])

    def from_quarter(values):
        return swap(jnp.tile(values, (sections,) + (1,) * (values.ndim - 1)), "pipe")

    first = first_factor[0].reshape(blocks, block_size, expand, ranks, cols)
    first = first.transpose(3, 0, 2, 4, 1).reshape(ranks, blocks, inner, block_size)
    fourth = fourth_factor[0].reshape(blocks, expand, ranks, cols, block_size)
    fourth = fourth.transpose(2, 0, 1, 3, 4).reshape(ranks, blocks, inner, block_size)
    outer = quarters(swap(jnp.stack([first, fourth], axis=1), "tensor"))
    second = quarters(second_factor[0])
    third = quarters(third_factor[0])
    weights = []
    for layer in range(sections):
        own = (outer[layer], second[layer], third[layer])
        if weights:
            own, weights[-1] = lax.optimization_barrier((own, weights[-1]))
        weights.append(tuple(from_quarter(member) for member in own))
    outer_shape = (all_blocks, inner, block_size)
    factors = [
        (w[0][:, 0].reshape(outer_shape), w[1], w[2], w[0][:, 1].reshape(outer_shape))
        for w in weights
    ]

    streams = whole_stream(inputs)
    grads = whole_stream(cotangent)
    gains = lax.all_gather(norm_gain[0], "tensor", axis=0, tiled=True)
    gains = lax.all_gather(gains, "pipe", axis=0, tiled=False)

    def forward(layer, stream):
        first, second, third, fourth = factors[layer]
        f = stream.astype(F32)
        inv = lax.rsqrt(jnp.mean(f * f, axis=0) + EPS)
        normed = (f * inv * gains[layer][:, None]).astype(BF16)
        normed = normed.reshape(all_blocks, block_size, tokens)
        spread = to_cols(dot("ikj,ijt->ikt", first, normed).astype(BF16))
        preact = dot("cme,cmt->cet", second, spread)
        act = gelu_value(preact).astype(BF16)
        mixed = to_blocks(dot("cem,cet->cmt", third, act).astype(BF16))
        branch = dot("ikj,ikt->ijt", fourth, mixed).astype(BF16)
        return branch.reshape(width, tokens), (stream, inv, normed, spread, preact, act, mixed)

    records = [[None] * share for _ in range(sections)]
    outs = [[None] * share for _ in range(sections)]
    for layer in range(sections):
        for k in range(share):
            if layer:
                former = streams[k]
                total = waiting[k].astype(F32)
                streams[k] = (former.astype(F32) + total).astype(BF16)
                outs[layer - 1][k] = my_rows(streams[k])
            branch, records[layer][k] = forward(layer, streams[k])
            start_sum(k, branch, layer == sections - 1)

    def close_forward(k):
        outs[-1][k] = (my_rows(streams[k]).astype(F32) + waiting[k].astype(F32)).astype(BF16)

    def backward(layer, k):
        first, second, third, fourth = factors[layer]
        stream, inv, normed, spread, preact, act, mixed = records[layer][k]
        grad_blocks = grads[k].reshape(all_blocks, block_size, tokens)
        part_four = dot("ikt,ijt->ikj", mixed, grad_blocks)
        grad_mixed = to_cols(dot("ikj,ijt->ikt", fourth, grad_blocks).astype(BF16))
        part_three = dot("cet,cmt->cem", act, grad_mixed)
        grad_act = dot("cem,cmt->cet", third, grad_mixed)
        grad_pre = (grad_act * gelu_slope(preact)).astype(BF16)
        part_two = dot("cmt,cet->cme", spread, grad_pre)
        grad_spread = to_blocks(dot("cme,cet->cmt", second, grad_pre).astype(BF16))
        part_one = dot("ikt,ijt->ikj", grad_spread, normed)
        grad_norm = dot("ikj,ikt->ijt", first, grad_spread).astype(BF16)
        return grad_norm.reshape(width, tokens), (part_one, part_two, part_three, part_four)

    def norm_backward(layer, k, grad_out, grad_norm, inner_sum):
        stream, inv = records[layer][k][:2]
        gain = gains[layer]
        if inner_sum is not None:
            stream, gain = my_rows(stream), my_rows(gain)
        f = stream.astype(F32)
        grad_norm = grad_norm.astype(F32)
        scaled = grad_norm * gain[:, None]
        if inner_sum is None:
            inner_sum = jnp.sum(scaled * f, axis=0)
        result = (
            grad_out.astype(F32) + scaled * inv - f * (inv * inv * inv * inner_sum / width)
        ).astype(BF16)
        if stream.shape[0] != width_dev:
            grad_norm, f = my_rows(grad_norm), my_rows(stream).astype(F32)
        return result, jnp.sum(grad_norm * f * inv, axis=1)

    back = [[None] * share for _ in range(sections)]
    gain_parts = [0.0] * sections
    sums = [None] * sections
    inner_sums = None
    for layer in reversed(range(sections)):
        parts = []
        inner_parts = []
        for k in range(share):
            if layer == sections - 1:
                close_forward(k)
            else:
                grads[k], part_gain = norm_backward(layer + 1, k, grads[k], waiting[k], None)
                gain_parts[layer + 1] += part_gain
                back[layer + 1][k] = my_rows(grads[k])
            grad_norm, part = backward(layer, k)
            parts.append(part)
            if layer == 0:
                scaled = grad_norm.astype(F32) * gains[0][:, None]
                inner_parts.append(jnp.sum(scaled * records[0][k][0].astype(F32), axis=0))
            start_sum(k, grad_norm, layer == 0)
        if layer == 0:
            inner_sums = lax.psum(jnp.stack(inner_parts), "tensor")
        part_one, part_two, part_three, part_four = (sum(member) for member in zip(*parts))
        shape = (ranks, blocks, inner, block_size)
        ends = jnp.stack([part_one.reshape(shape), part_four.reshape(shape)], axis=1)
        sums[layer] = tuple(
            jnp.sum(quarters(member.astype(BF16)).astype(F32), axis=0).astype(BF16)
            for member in (ends, part_two, part_three)
        )
    for k in range(share):
        back[0][k], part_gain = norm_backward(0, k, my_rows(grads[k]), waiting[k], inner_sums[k])
        gain_parts[0] += part_gain

    def placed(members):
        moved = swap(jnp.stack([jnp.stack(row) for row in members]), "pipe")
        moved = moved.reshape(micro_count, width_dev, tokens)
        return moved.transpose(0, 2, 1)[None]

    def collected(which):
        moved = swap(jnp.stack([member[which] for member in sums]), "pipe")
        return moved.reshape((-1,) + moved.shape[2:])

    gain_grad = jnp.sum(swap(jnp.stack(gain_parts), "pipe"), axis=0)
    ends = swap(collected(0), "tensor")
    ends = ends.reshape(ranks, 2, blocks, expand, cols, block_size).astype(F32)
    first_grad = ends[:, 0].transpose(1, 4, 2, 0, 3)
    fourth_grad = ends[:, 1].transpose(1, 2, 0, 3, 4)
    return (
        placed(outs),
        placed(back),
        gain_grad[None],
        first_grad.reshape(1, blocks, block_size, expand * block_size),
        collected(1).astype(F32)[None],
        collected(2).astype(F32)[None],
        fourth_grad.reshape(1, blocks, expand * block_size, block_size),
    )


def solution(mesh):
    factor = P("pipe", "tensor", None, None)
    stream = P(None, None, "tensor")
    result = P("pipe", None, None, "tensor")
    return jax.shard_map(
        body,
        mesh=mesh,
        in_specs=(stream, stream, P("pipe", "tensor"), factor, factor, factor, factor),
        out_specs=(result, result, P("pipe", "tensor"), factor, factor, factor, factor),
        check_vma=False,
    )
```

```python
import math

import jax
import jax.numpy as jnp
from jax import lax
from jax.experimental.layout import Layout, with_layout_constraint
from jax.sharding import Mesh
from jax.sharding import PartitionSpec as P

EPS = 1e-05
TANH_SCALE = math.sqrt(2.0 / math.pi)
CUBIC_COEF = 0.044715
F32 = jnp.float32
BF16 = jnp.bfloat16


TENSOR = ("chip", "core")


def gelu_value(preact):
    tanh_val = jnp.tanh(TANH_SCALE * (preact + CUBIC_COEF * preact * preact * preact))
    return 0.5 * preact * (1.0 + tanh_val)


def gelu_slope(preact):
    tanh_val = jnp.tanh(TANH_SCALE * (preact + CUBIC_COEF * preact * preact * preact))
    return 0.5 * (1.0 + tanh_val) + 0.5 * preact * (
        1.0 - tanh_val * tanh_val
    ) * TANH_SCALE * (1.0 + 3.0 * CUBIC_COEF * preact * preact)


def dot(spec, left, right):
    return jnp.einsum(spec, left, right, preferred_element_type=F32)


def swap(values, axis):
    return lax.all_to_all(values, axis, split_axis=0, concat_axis=0, tiled=True)


def body(inputs, cotangent, norm_gain, first_factor, second_factor, third_factor, fourth_factor):
    sections = lax.axis_size("pipe")
    group = lax.axis_index("pipe")
    ranks = lax.axis_size(TENSOR)
    rank = lax.axis_index(TENSOR)
    micro_count, tokens, width_dev = inputs.shape
    width = width_dev * ranks
    share = micro_count // sections
    blocks, block_size = first_factor.shape[1], first_factor.shape[2]
    expand = first_factor.shape[3] // block_size
    cols, mix_width = second_factor.shape[1], second_factor.shape[2]
    all_blocks = mix_width // expand
    inner = expand * cols

    def rows_first(values):
        return with_layout_constraint(values, Layout(major_to_minor=(0, 1)))

    def whole_stream(values):
        mine = lax.dynamic_slice_in_dim(values, group * share, share, 0)
        mine = mine.reshape(share * tokens, width_dev).T
        full = rows_first(lax.all_gather(rows_first(mine), TENSOR, axis=0, tiled=True))
        return [full[:, k * tokens : (k + 1) * tokens] for k in range(share)]

    def to_cols(values):
        return (
            values.reshape(all_blocks, expand, cols, tokens)
            .transpose(2, 0, 1, 3)
            .reshape(cols, mix_width, tokens)
        )

    def to_blocks(values):
        return (
            values.reshape(cols, all_blocks, expand, tokens)
            .transpose(1, 2, 0, 3)
            .reshape(all_blocks, inner, tokens)
        )

    def my_rows(values):
        return lax.dynamic_slice_in_dim(values, rank * width_dev, width_dev, 0)

    waiting = [None] * share
    newest = [None]

    core = lax.axis_index("core")
    chips = lax.axis_size("chip")

    def from_other_core(values):
        return lax.ppermute(values, "core", [(0, 1), (1, 0)])

    def start_sum(k, partial, scatter, riders=()):
        halves = partial.reshape(chips, 2, width_dev, tokens)
        kept = lax.dynamic_index_in_dim(halves, core, 1, keepdims=False)
        sent = lax.dynamic_index_in_dim(halves, 1 - core, 1, keepdims=False)
        kept = (kept.astype(F32) + from_other_core(sent).astype(F32)).astype(BF16)
        kept = kept.reshape(chips * width_dev, tokens)
        if newest[0] is not None:
            last = newest[0]
            kept, waiting[last], riders = lax.optimization_barrier((kept, waiting[last], riders))
        if scatter:
            waiting[k] = lax.psum_scatter(kept, "chip", scatter_dimension=0, tiled=True)
        else:
            waiting[k] = rows_first(lax.psum(kept, "chip"))
        newest[0] = k
        return riders

    def finished(k):
        mine = waiting[k].reshape(chips, width_dev, tokens)
        other = from_other_core(mine)
        is_even = core == 0
        both = (jnp.where(is_even, mine, other), jnp.where(is_even, other, mine))
        return jnp.stack(both, axis=1).reshape(width, tokens)

    def quarters(values):
        moved = swap(values, "pipe")
        return moved.reshape((sections, moved.shape[0] // sections) + moved.shape[1:])

    def from_quarter(values):
        return swap(jnp.tile(values, (sections,) + (1,) * (values.ndim - 1)), "pipe")

    first = first_factor[0].reshape(blocks, block_size, expand, ranks, cols)
    first = first.transpose(3, 0, 2, 4, 1).reshape(ranks, blocks, inner, block_size)
    fourth = fourth_factor[0].reshape(blocks, expand, ranks, cols, block_size)
    fourth = fourth.transpose(2, 0, 1, 3, 4).reshape(ranks, blocks, inner, block_size)
    outer = quarters(swap(jnp.stack([first, fourth], axis=1), TENSOR))
    second = quarters(second_factor[0])
    third = quarters(third_factor[0])
    weights = []
    for layer in range(sections):
        own = (outer[layer], second[layer], third[layer])
        if weights:
            own, weights[-1] = lax.optimization_barrier((own, weights[-1]))
        weights.append(tuple(from_quarter(member) for member in own))
    outer_shape = (all_blocks, inner, block_size)
    factors = [
        (w[0][:, 0].reshape(outer_shape), w[1], w[2], w[0][:, 1].reshape(outer_shape))
        for w in weights
    ]

    streams = whole_stream(inputs)
    grads = whole_stream(cotangent)
    gains = lax.all_gather(norm_gain[0], ("pipe",) + TENSOR, axis=0, tiled=True)
    gains = gains.reshape(sections, width)

    def forward(layer, stream):
        first, second, third, fourth = factors[layer]
        f = stream.astype(F32)
        inv = lax.rsqrt(jnp.mean(f * f, axis=0) + EPS)
        normed = (f * inv * gains[layer][:, None]).astype(BF16)
        normed = normed.reshape(all_blocks, block_size, tokens)
        spread = to_cols(dot("ikj,ijt->ikt", first, normed).astype(BF16))
        preact = dot("cme,cmt->cet", second, spread)
        act = gelu_value(preact).astype(BF16)
        mixed = to_blocks(dot("cem,cet->cmt", third, act).astype(BF16))
        branch = dot("ikj,ikt->ijt", fourth, mixed).astype(BF16)
        return branch.reshape(width, tokens), (stream, inv, normed, spread, preact, act, mixed)

    records = [[None] * share for _ in range(sections)]
    outs = [[None] * share for _ in range(sections)]
    for layer in range(sections):
        for k in range(share):
            if layer:
                former = streams[k]
                total = finished(k).astype(F32)
                streams[k] = (former.astype(F32) + total).astype(BF16)
                outs[layer - 1][k] = my_rows(streams[k])
            branch, records[layer][k] = forward(layer, streams[k])
            start_sum(k, branch, layer == sections - 1)

    def close_forward(k):
        outs[-1][k] = (my_rows(streams[k]).astype(F32) + waiting[k].astype(F32)).astype(BF16)

    def backward(layer, k):
        first, second, third, fourth = factors[layer]
        stream, inv, normed, spread, preact, act, mixed = records[layer][k]
        grad_blocks = grads[k].reshape(all_blocks, block_size, tokens)
        part_four = dot("ikt,ijt->ikj", mixed, grad_blocks)
        grad_mixed = to_cols(dot("ikj,ijt->ikt", fourth, grad_blocks).astype(BF16))
        part_three = dot("cet,cmt->cem", act, grad_mixed)
        grad_act = dot("cem,cmt->cet", third, grad_mixed)
        grad_pre = (grad_act * gelu_slope(preact)).astype(BF16)
        part_two = dot("cmt,cet->cme", spread, grad_pre)
        grad_spread = to_blocks(dot("cme,cet->cmt", second, grad_pre).astype(BF16))
        part_one = dot("ikt,ijt->ikj", grad_spread, normed)
        grad_norm = dot("ikj,ikt->ijt", first, grad_spread).astype(BF16)
        return grad_norm.reshape(width, tokens), (part_one, part_two, part_three, part_four)

    def norm_backward(layer, k):
        stream, inv = records[layer][k][:2]
        f = stream.astype(F32)
        grad_norm = finished(k).astype(F32)
        scaled = grad_norm * gains[layer][:, None]
        inner_sum = jnp.sum(scaled * f, axis=0)
        grads[k] = (
            grads[k].astype(F32) + scaled * inv - f * (inv * inv * inv * inner_sum / width)
        ).astype(BF16)
        back[layer][k] = my_rows(grads[k])
        gain_parts[layer] += jnp.sum(my_rows(grad_norm) * my_rows(stream).astype(F32) * inv, axis=1)

    back = [[None] * share for _ in range(sections)]
    gain_parts = [0.0] * sections
    sums = [()] * (sections + 1)
    for layer in reversed(range(sections)):
        parts = []
        for k in range(share):
            if layer == sections - 1:
                close_forward(k)
            else:
                norm_backward(layer + 1, k)
            grad_norm, part = backward(layer, k)
            parts.append(part)
            if k == share - 1:
                sums[layer + 1] = start_sum(k, grad_norm, False, sums[layer + 1])
            else:
                start_sum(k, grad_norm, False)
        part_one, part_two, part_three, part_four = (sum(member) for member in zip(*parts))
        shape = (ranks, blocks, inner, block_size)
        ends = jnp.stack([part_one.reshape(shape), part_four.reshape(shape)], axis=1)
        sums[layer] = tuple(
            jnp.sum(quarters(member.astype(BF16)).astype(F32), axis=0).astype(BF16)
            for member in (ends, part_two, part_three)
        )
    sums = sums[:sections]
    for k in range(share):
        norm_backward(0, k)

    def placed(members):
        moved = swap(jnp.stack([jnp.stack(row) for row in members]), "pipe")
        moved = moved.reshape(micro_count, width_dev, tokens)
        return moved.transpose(0, 2, 1)[None]

    def collected(which):
        moved = swap(jnp.stack([member[which] for member in sums]), "pipe")
        return moved.reshape((-1,) + moved.shape[2:])

    gain_grad = jnp.sum(swap(jnp.stack(gain_parts), "pipe"), axis=0)
    ends = swap(collected(0), TENSOR)
    ends = ends.reshape(ranks, 2, blocks, expand, cols, block_size).astype(F32)
    first_grad = ends[:, 0].transpose(1, 4, 2, 0, 3)
    fourth_grad = ends[:, 1].transpose(1, 2, 0, 3, 4)
    return (
        placed(outs),
        placed(back),
        gain_grad[None],
        first_grad.reshape(1, blocks, block_size, expand * block_size),
        collected(1).astype(F32)[None],
        collected(2).astype(F32)[None],
        fourth_grad.reshape(1, blocks, expand * block_size, block_size),
    )


def solution(mesh):
    pipes, ranks = mesh.shape["pipe"], mesh.shape["tensor"]
    split = Mesh(mesh.devices.reshape(pipes, ranks // 2, 2), ("pipe",) + TENSOR)
    factor = P("pipe", TENSOR, None, None)
    stream = P(None, None, TENSOR)
    result = P("pipe", None, None, TENSOR)
    return jax.shard_map(
        body,
        mesh=split,
        in_specs=(stream, stream, P("pipe", TENSOR), factor, factor, factor, factor),
        out_specs=(result, result, P("pipe", TENSOR), factor, factor, factor, factor),
        check_vma=False,
    )
```
